32 devices in a mesh: slab: 16 (over z, y, x), dp: 2 (over core).
Axes of the slice: x: 2, y: 2, z: 4, core: 2. Of those that a mesh axis runs over, the one named last changes fastest.
Arguments:
- field: bfloat16 [2, 64, 32, 64, 512], P('dp', 'slab'), may hold values from -6 to 6
- cotangent: bfloat16 [2, 64, 32, 64, 512], P('dp', 'slab'), may hold values from -6 to 6
- spectral_weight: bfloat16 [96, 16, 16, 32, 64], P('slab'), may hold values from -9 to 9
- point_weight: bfloat16 [32, 32], replicated, may hold values from -1 to 1
- bias_term: float32 [32], replicated, may hold values from -3 to 3
Outputs:
- layer_out: bfloat16 [2, 64, 32, 64, 512], P('dp', 'slab')
- field_grad: bfloat16 [2, 64, 32, 64, 512], P('dp', 'slab')
- weight_grad: float32 [96, 16, 16, 32, 64], P('slab')
The draws below stay inside these ranges and needn't reach their ends.
All inputs are finite; a program needn't handle non-finite values.
Results may differ from the reference program's by a relative error of at most 0.018.
Values may be sent and summed in bfloat16 or wider, within the bound.
A program may use at most 192 MiB of HBM per device.

```python
import math
from functools import partial
import jax
import jax.numpy as jnp
from jax import lax

X = 64
Y = 64
Z = 32
T_SIZE = 16
C = 32
MX = 16
MY = 16
MZ = 12
MT = 8
ZT = 512
KZT = 96
SAMPLES = 2


def levels(rng, extent, split, least, largest):
    loudness, own = 1.0, jax.random.fold_in(rng, 6)
    for position, blocks in split:
        heights = jnp.exp(jax.random.uniform(jax.random.fold_in(own, position), (blocks,), jnp.float32, least / len(split), largest / len(split)))
        loudness = loudness * jnp.repeat(heights, extent[position] // blocks).reshape([-1 if axis == position else 1 for axis in range(len(extent))])
    return loudness


def noise(key, dims, deviation, most, shards=(), kind=jnp.bfloat16):
    array = jax.random.normal(key, dims, jnp.float32) * deviation
    if len(shards) > 0:
        array = levels(key, dims, shards, -0.22, 0.18) * array
    return jnp.clip(array, min=-most, max=most).astype(kind)


def setup_inputs(seed: int = 0) -> dict:
    seeds = jax.random.split(jax.random.key(seed), 6)
    return {
        "field": noise(seeds[0], (SAMPLES, X, C, Y, ZT), 1.0, 6.0, ((0, 2), (1, 16))),
        "cotangent": noise(seeds[1], (SAMPLES, X, C, Y, ZT), 1.0, 6.0, ((0, 2), (1, 16))),
        "spectral_weight": noise(seeds[2], (KZT, MX, MY, C, 2 * C), 1.5, 9.0, ((0, 16),)),
        "point_weight": noise(seeds[3], (C, C), C ** -0.5, 1.0),
        "bias_term": noise(seeds[4], (C,), 0.5, 3.0, (), jnp.float32),
    }


def signed_freq(index, modes):
    return jnp.where(index < modes // 2, index, index - modes)

def inner_table():
    freq = jnp.arange(MZ * MT, dtype=jnp.int32)
    place = jnp.arange(Z * T_SIZE, dtype=jnp.int32)
    kdepth = (signed_freq(freq // MT, MZ) % Z)[:, None]
    ktime = (freq % MT)[:, None]
    zdepth = (place // T_SIZE)[None, :]
    tlevel = (place % T_SIZE)[None, :]
    counts = kdepth * zdepth % Z * T_SIZE + ktime * tlevel % T_SIZE * Z
    angle = 2.0 * math.pi / (Z * T_SIZE) * (counts % (Z * T_SIZE)).astype(jnp.float32)
    return jnp.stack([jnp.cos(angle), -jnp.sin(angle)]).astype(jnp.bfloat16)

def complex_table(modes, length):
    kpos = (signed_freq(jnp.arange(modes, dtype=jnp.int32), modes) % length)[:, None]
    jpos = jnp.arange(length, dtype=jnp.int32)[None, :]
    angle = 2.0 * math.pi / length * (kpos * jpos % length).astype(jnp.float32)
    cosine = jnp.cos(angle)
    sine = jnp.sin(angle)
    first = jnp.stack([cosine, sine], axis=1)
    second = jnp.stack([-sine, cosine], axis=1)
    return jnp.stack([first, second]).astype(jnp.bfloat16)

def contract(form, left, right):
    return jnp.einsum(form, left.astype(jnp.float32), right.astype(jnp.float32), precision=lax.Precision.HIGHEST)

def analyse(values, inner, middle, outer):
    first = contract('xcyt,pqt->xqpyc', values, inner).astype(jnp.bfloat16)
    second = contract('rkpy,xqpyc->xqrkc', middle, first).astype(jnp.bfloat16)
    return contract('rkpx,xqpyc->qkryc', outer, second)

def synthesise(spectrum, inner, middle, outer):
    first = contract('pkrx,qkpyc->xqryc', outer, spectrum).astype(jnp.bfloat16)
    second = contract('pkry,xqpkc->xqryc', middle, first).astype(jnp.bfloat16)
    return contract('xqpyc,pqt->xcyt', second, inner)

def pairs(grad_spec):
    real_part = grad_spec[..., 0, :, :]
    imag_part = grad_spec[..., 1, :, :]
    first = jnp.concatenate([real_part, imag_part], axis=-1)
    second = jnp.concatenate([imag_part, -real_part], axis=-1)
    return jnp.stack([first, second], axis=-3)

def mixing(spectrum, weights):
    both = contract('qkpyc,qkyco->qkpyo', spectrum, weights)
    real_part = both[:, :, 0, :, :C] - both[:, :, 1, :, C:]
    imag_part = both[:, :, 0, :, C:] + both[:, :, 1, :, :C]
    return jnp.stack([real_part, imag_part], axis=2).astype(jnp.bfloat16)

def one_sample(inputs, upstream, spectral_weight, point_weight, bias_term):
    inner = inner_table()
    middle = complex_table(MY, Y)
    outer = complex_table(MX, X)
    scale = 1.0 / (X * Y * Z * T_SIZE)
    spectrum = analyse(inputs, inner, middle, outer).astype(jnp.bfloat16)
    mixed = mixing(spectrum, spectral_weight)
    spectral = synthesise(mixed, inner, middle, outer) * scale
    linear = contract('oc,xcyt->xoyt', point_weight, inputs)
    preact = spectral + linear + bias_term[None, :, None, None]
    activation = partial(jax.nn.gelu, approximate=True)
    layer_out = activation(preact).astype(jnp.bfloat16)
    pulled = jax.vjp(activation, preact)[1](upstream.astype(preact.dtype))[0]
    grad_pre = pulled.astype(jnp.bfloat16)
    grad_spec = (analyse(grad_pre, inner, middle, outer) * scale).astype(jnp.bfloat16)
    spec_back = contract('qkyco,qkpyo->qkpyc', spectral_weight, pairs(grad_spec)).astype(jnp.bfloat16)
    total = synthesise(spec_back, inner, middle, outer) + contract('oc,xoyt->xcyt', point_weight, grad_pre)
    return (layer_out, total.astype(jnp.bfloat16), spectrum, grad_spec)

def reference(field, cotangent, spectral_weight, point_weight, bias_term):

    def per_sample(inputs):
        return one_sample(inputs[0], inputs[1], spectral_weight, point_weight, bias_term)
    layer_out, field_grad, spectra, grad_spectra = lax.map(per_sample, (field, cotangent))
    weight_grad = contract('sqkpyc,sqkpyo->qkyco', spectra, pairs(grad_spectra))
    return (layer_out, field_grad, weight_grad)
```

```python
from functools import partial

import jax
import jax.numpy as jnp
import ml_dtypes
import numpy as np
from jax import lax
from jax.experimental import pallas as pl
from jax.experimental.pallas import tpu as pltpu
from jax.sharding import PartitionSpec as P

X = 64
Z = 32
T_SIZE = 16
MZ = 12
MT = 8
PARTS = 2
LIMIT = 52 * 1024 * 1024
BF = jnp.bfloat16
F32 = jnp.float32
NT = (((1,), (1,)), ((), ()))
TN = (((0,), (0,)), ((), ()))


def signed(m):
    i = np.arange(m)
    return np.where(i < m // 2, i, i - m)


def rounded(a):
    return np.asarray(a, np.float32).astype(ml_dtypes.bfloat16)


def waves(modes, length):
    angle = 2.0 * np.pi / length * ((signed(modes)[:, None] * np.arange(length)[None, :]) % length)
    return np.cos(angle), np.sin(angle)


def zt_waves():
    q = np.arange(MZ * MT)
    t = np.arange(Z * T_SIZE)
    total = Z * T_SIZE
    counts = (signed(MZ)[q // MT][:, None] * (t // T_SIZE)[None, :] * T_SIZE
              + (q % MT)[:, None] * (t % T_SIZE)[None, :] * Z) % total
    angle = 2.0 * np.pi / total * counts
    return np.cos(angle), -np.sin(angle)


class Tables:
    def __init__(self, n, xl, c, y, ql, mx, my, parts):
        xs = xl // parts
        i0, i1 = zt_waves()
        rows = np.arange(n * 2 * ql)
        dest, r, j = rows // (2 * ql), rows // ql % 2, rows % ql
        q = dest * ql + j
        first = np.where(r[:, None] == 0, i0[q], i1[q])
        second = np.where(r[:, None] == 0, i1[q], -i0[q])
        self.inner = rounded(np.concatenate([first, second], axis=1))
        cos, sin = waves(my, y)
        g = 4
        eye = np.eye(g)
        self.ya = rounded(np.stack([
            np.einsum("ab,ky->akby", eye, w).reshape(g * my, g * y) for w in (cos, sin)
        ]).reshape(2 * g * my, g * y))
        g = 8
        eye = np.eye(g)
        self.ys = rounded(np.concatenate([
            np.einsum("ab,ky->aybk", eye, w).reshape(g * y, g * my) for w in (cos, sin)
        ], axis=1))
        k = n * xs * 2 * ql
        out = np.arange(k)
        d, rest = out // (xs * 2 * ql), out % (xs * 2 * ql)
        x, w = rest // (2 * ql), rest % (2 * ql)
        src = (x * n + d) * 2 * ql + w
        perm = np.zeros((k, k))
        perm[out, src] = 1
        self.perm = rounded(perm)
        self.perm_t = rounded(perm.T)
        cx, sx = waves(mx, n * xl)
        big = np.zeros((2, 2, mx, n * xl))
        big[0, 0], big[0, 1], big[1, 0], big[1, 1] = cx, sx, -sx, cx
        full = np.einsum("rpkx,qj->qkrxpj", big, np.eye(ql))
        full = full.reshape(ql * mx * 2, n, parts, xs * 2 * ql)
        self.xa = rounded(full.transpose(2, 0, 1, 3).reshape(parts, ql * mx * 2, k))
        self.xs = rounded(full.transpose(2, 1, 3, 0).reshape(parts, k, ql * mx * 2))
        lanes = np.arange(c * my)
        swap = np.zeros((c * my, c * my))
        swap[lanes, lanes % my * c + lanes // my] = 1
        self.swap = rounded(swap)
        self.swap_t = rounded(swap.T)
        tile = np.zeros((c, c * my))
        tile[lanes // my, lanes] = 1
        self.tile = rounded(tile)
        spread = np.zeros((mx * 2 * my, mx * 2))
        spread[np.arange(mx * 2 * my), np.arange(mx * 2 * my) // my] = 1
        self.spread = rounded(spread)
        h = 16
        rep = np.zeros((c * h, c))
        rep[np.arange(c * h), np.arange(c * h) // h] = 1
        self.rep = rounded(rep)


def dot(a, b, dims=None):
    if dims is None:
        return jnp.dot(a, b, preferred_element_type=F32)
    return lax.dot_general(a, b, dims, preferred_element_type=F32)


def whole(a):
    return pl.BlockSpec(a.shape, lambda *_: (0,) * a.ndim)


def analyse_plane(load, ya, inner, v_ref, c, y, my):
    zt = inner.shape[1] // 2
    for g in range(c // 4):
        out = dot(ya[...], load(g).reshape(4 * y, zt)).astype(BF)
        v_ref[4 * my * g:4 * my * (g + 1), :zt] = out[:4 * my]
        v_ref[4 * my * g:4 * my * (g + 1), zt:] = out[4 * my:]
    return dot(inner[...], v_ref[...], NT).astype(BF)


def analyse_kernel(field, ya, inner, perm, out, v_ref, all_ref):
    i, steps = pl.program_id(0), pl.num_programs(0)
    c, y = field.shape[2:4]
    my = v_ref.shape[0] // c
    rows = inner.shape[0]
    spec = analyse_plane(lambda g: field[0, 0, 4 * g:4 * g + 4], ya, inner, v_ref, c, y, my)
    all_ref[pl.ds(pl.multiple_of(i * rows, rows), rows), :] = spec

    @pl.when(i == steps - 1)
    def _():
        out[...] = dot(perm[...], all_ref[...]).astype(BF)


def params():
    return pltpu.CompilerParams(vmem_limit_bytes=LIMIT)


def analyse(field, tab, part, xs, my):
    _, _, c, y, zt = field.shape
    rows = tab.inner.shape[0]
    args = [jnp.asarray(tab.ya), jnp.asarray(tab.inner), jnp.asarray(tab.perm)]
    return pl.pallas_call(
        analyse_kernel,
        grid=(xs,),
        in_specs=[pl.BlockSpec((1, 1, c, y, zt), lambda i: (0, part * xs + i, 0, 0, 0))] + [whole(a) for a in args],
        out_specs=pl.BlockSpec((xs * rows, c * my), lambda i: (0, 0)),
        out_shape=jax.ShapeDtypeStruct((xs * rows, c * my), BF),
        scratch_shapes=[pltpu.VMEM((c * my, 2 * zt), BF), pltpu.VMEM((xs * rows, c * my), BF)],
        compiler_params=params(),
        name="analyse",
    )(field, *args)


def row_mask(rows, lanes, my, by_minor, c):
    row = lax.broadcasted_iota(jnp.int32, (rows, lanes), 0) % my
    lane = lax.broadcasted_iota(jnp.int32, (rows, lanes), 1)
    return row == (lane % my if by_minor else lane // c)


def mix_kernel(parts, my, scale, *refs):
    recv = refs[:parts]
    w, xa, xs, swap, tile, spread = refs[parts:parts + 6]
    outs = refs[parts + 6:2 * parts + 6]
    spec_out, spec, mixed, both = refs[2 * parts + 6:]
    i, steps = pl.program_id(0), pl.num_programs(0)
    c, mx = w.shape[3], w.shape[1]
    lanes = c * my

    @pl.when(i == 0)
    def _():
        total = dot(xa[0], recv[0][...])
        for p in range(1, parts):
            total += dot(xa[p], recv[p][...])
        spec[...] = dot(total.astype(BF), swap[...]).astype(BF)
        spec_out[...] = spec[...]

    here = pl.ds(pl.multiple_of(i * mx * 2, mx * 2), mx * 2)
    rep = dot(spread[...], spec[here, :])
    block = jnp.where(row_mask(mx * 2 * my, lanes, my, False, c), rep, 0.0).astype(BF)
    for k in range(mx):
        both[2 * my * k:2 * my * (k + 1), :] = dot(
            block[2 * my * k:2 * my * (k + 1)], w[0, k].reshape(lanes, 2 * c))
    b = both[...].reshape(mx, 2, my, 2 * c)
    b0, b1 = b[:, 0], b[:, 1]
    real = b0[..., :c] - b1[..., c:]
    imag = b0[..., c:] + b1[..., :c]
    small = jnp.stack([real, imag], axis=1).reshape(mx * 2 * my, c).astype(BF)
    wide = dot(small, tile[...])
    wide = jnp.where(row_mask(mx * 2 * my, lanes, my, True, c), wide, 0.0).astype(BF)
    mixed[here, :] = dot(spread[...], wide, TN).astype(BF)

    @pl.when(i == steps - 1)
    def _():
        for p in range(parts):
            outs[p][...] = (dot(xs[p], mixed[...]) * scale).astype(BF)


def mix(recv, weight, tab, my, scale):
    parts = len(recv)
    ql, mx, _, c, _ = weight.shape
    lanes = c * my
    args = [jnp.asarray(a) for a in (tab.xa, tab.xs, tab.swap, tab.tile, tab.spread)]
    rows = ql * mx * 2
    out_shape = [jax.ShapeDtypeStruct(r.shape, BF) for r in recv] + [jax.ShapeDtypeStruct((rows, lanes), BF)]
    return pl.pallas_call(
        partial(mix_kernel, parts, my, scale),
        grid=(ql,),
        in_specs=[whole(r) for r in recv]
        + [pl.BlockSpec((1, mx, my, c, 2 * c), lambda i: (i, 0, 0, 0, 0))]
        + [whole(a) for a in args],
        out_specs=[whole(a) for a in out_shape],
        out_shape=out_shape,
        scratch_shapes=[pltpu.VMEM((rows, lanes), BF), pltpu.VMEM((rows, lanes), BF),
                        pltpu.VMEM((mx * 2 * my, 2 * c), F32)],
        compiler_params=params(),
        name="mix",
    )(*recv, weight, *args)


def pair_rows(g, tile, spread, mask, mx, my, c):
    rep = jnp.where(mask, dot(spread[...], g), 0.0).astype(BF)
    small = dot(rep, tile[...], NT).reshape(mx, 2, my, c)
    real, imag = small[:, 0], small[:, 1]
    first = jnp.concatenate([real, imag], axis=-1)
    second = jnp.concatenate([imag, -real], axis=-1)
    return jnp.stack([first, second], axis=1).reshape(mx * 2 * my, 2 * c).astype(BF)


def back_kernel(parts, my, scale, *refs):
    recv = refs[:parts]
    w, xa, xs, swap_t, tile, spread = refs[parts:parts + 6]
    outs = refs[parts + 6:2 * parts + 6]
    spec_out, spec, mixed, wide = refs[2 * parts + 6:]
    i, steps = pl.program_id(0), pl.num_programs(0)
    c, mx = w.shape[3], w.shape[1]
    lanes = c * my

    @pl.when(i == 0)
    def _():
        total = dot(xa[0], recv[0][...])
        for p in range(1, parts):
            total += dot(xa[p], recv[p][...])
        spec[...] = (total * scale).astype(BF)
        spec_out[...] = spec[...]

    here = pl.ds(pl.multiple_of(i * mx * 2, mx * 2), mx * 2)
    mask = row_mask(mx * 2 * my, lanes, my, True, c)
    pair = pair_rows(spec[here, :], tile, spread, mask, mx, my, c)
    block = row_mask(2 * my, lanes, my, False, c)
    for k in range(mx):
        out = dot(pair[2 * my * k:2 * my * (k + 1)], w[0, k].reshape(lanes, 2 * c), NT)
        wide[2 * my * k:2 * my * (k + 1), :] = jnp.where(block, out, 0.0).astype(BF)
    mixed[here, :] = dot(spread[...], wide[...], TN).astype(BF)

    @pl.when(i == steps - 1)
    def _():
        turned = dot(mixed[...], swap_t[...]).astype(BF)
        for p in range(parts):
            outs[p][...] = dot(xs[p], turned).astype(BF)


def back(recv, weight, tab, my, scale):
    parts = len(recv)
    ql, mx, _, c, _ = weight.shape
    lanes = c * my
    args = [jnp.asarray(a) for a in (tab.xa, tab.xs, tab.swap_t, tab.tile, tab.spread)]
    rows = ql * mx * 2
    out_shape = [jax.ShapeDtypeStruct(r.shape, BF) for r in recv] + [jax.ShapeDtypeStruct((rows, lanes), BF)]
    return pl.pallas_call(
        partial(back_kernel, parts, my, scale),
        grid=(ql,),
        in_specs=[whole(r) for r in recv]
        + [pl.BlockSpec((1, mx, my, c, 2 * c), lambda i: (i, 0, 0, 0, 0))]
        + [whole(a) for a in args],
        out_specs=[whole(a) for a in out_shape],
        out_shape=out_shape,
        scratch_shapes=[pltpu.VMEM((rows, lanes), BF), pltpu.VMEM((rows, lanes), BF),
                        pltpu.VMEM((mx * 2 * my, lanes), BF)],
        compiler_params=params(),
        name="back",
    )(*recv, weight, *args)


def weight_kernel(samples, my, *refs):
    specs, grads = refs[:samples], refs[samples:2 * samples]
    tile, spread, out = refs[2 * samples:]
    mx, c = out.shape[1], out.shape[3]
    lanes = c * my
    rows = mx * 2 * my
    minor = row_mask(rows, lanes, my, True, c)
    major = row_mask(rows, lanes, my, False, c)
    blocks, pairs = [], []
    for s in range(samples):
        blocks.append(jnp.where(major, dot(spread[...], specs[s][...]), 0.0).astype(BF))
        pairs.append(pair_rows(grads[s][...], tile, spread, minor, mx, my, c))
    for k in range(mx):
        cut = slice(2 * my * k, 2 * my * (k + 1))
        left = jnp.concatenate([b[cut] for b in blocks], axis=0)
        right = jnp.concatenate([b[cut] for b in pairs], axis=0)
        out[0, k] = dot(left, right, TN).reshape(my, c, 2 * c)


def weight_gradient(specs, grads, shape, tab):
    ql, mx, my, c, _ = shape
    lanes = c * my
    args = [jnp.asarray(tab.tile), jnp.asarray(tab.spread)]
    block = pl.BlockSpec((mx * 2, lanes), lambda i: (i, 0))
    return pl.pallas_call(
        partial(weight_kernel, len(specs), my),
        grid=(ql,),
        in_specs=[block] * (2 * len(specs)) + [whole(a) for a in args],
        out_specs=pl.BlockSpec((1, mx, my, c, 2 * c), lambda i: (i, 0, 0, 0, 0)),
        out_shape=jax.ShapeDtypeStruct(shape, F32),
        compiler_params=params(),
        name="weight_gradient",
    )(*specs, *grads, *args)


def expand_point(point, rep, kron, transposed):
    half = dot(rep[...], point[...], (((1,), (0 if not transposed else 1,)), ((), ()))).astype(BF)
    full = dot(half, rep[...], NT)
    n = full.shape[0]
    row = lax.broadcasted_iota(jnp.int32, (n, n), 0) % 16
    lane = lax.broadcasted_iota(jnp.int32, (n, n), 1) % 16
    kron[...] = jnp.where(row == lane, full, 0.0).astype(BF)


def linear_plane(load, kron, acc, c, y):
    for j in range(y // 16):
        block = load(j)
        zt = block.shape[-1]
        acc[:, 16 * j:16 * j + 16, :] = dot(kron[...], block.reshape(c * 16, zt)).reshape(c, 16, zt)


def synth_group(g, v, ys, my, zt):
    rows = 8 * my
    cut = slice(rows * g, rows * (g + 1))
    both = jnp.concatenate([v[cut, :zt], v[cut, zt:]], axis=0)
    return dot(ys[...], both)


def forward_kernel(aliased, field, cot, recv, ys, ya, inner, perm, perm_t, rep, point, bias, *refs):
    if aliased:
        refs = refs[1:]
    layer, grad, out, all_in, all_out, v_ref, kron, acc = refs
    i, steps = pl.program_id(0), pl.num_programs(0)
    c, y, zt = field.shape[2:]
    my = v_ref.shape[0] // c
    rows = inner.shape[0]

    @pl.when(i == 0)
    def _():
        all_in[...] = dot(perm_t[...], recv[...]).astype(BF)
        expand_point(point, rep, kron, False)

    here = pl.ds(pl.multiple_of(i * rows, rows), rows)
    v_ref[...] = dot(all_in[here, :], inner[...], TN).astype(BF)
    linear_plane(lambda j: field[0, 0, :, 16 * j:16 * j + 16, :], kron, acc, c, y)
    k0 = float(np.sqrt(2.0 / np.pi))
    k1 = k0 * 0.044715
    for g in range(c // 8):
        spectral = synth_group(g, v_ref, ys, my, zt)
        for h in range(8):
            ch = 8 * g + h
            pre = spectral[y * h:y * (h + 1)] + (acc[ch] + bias[ch])
            sq = pre * pre
            th = jnp.tanh(pre * (k0 + k1 * sq))
            cdf = 0.5 + 0.5 * th
            layer[0, 0, ch] = (pre * cdf).astype(BF)
            slope = cdf + (0.5 * pre) * ((1.0 - th * th) * (k0 + (3.0 * k1) * sq))
            grad[0, ch] = (cot[0, 0, ch].astype(F32) * slope).astype(BF)
    all_out[here, :] = analyse_plane(lambda g: grad[0, 4 * g:4 * g + 4], ya, inner, v_ref, c, y, my)

    @pl.when(i == steps - 1)
    def _():
        out[...] = dot(perm[...], all_out[...]).astype(BF)


def forward(field, cot, recv, point, bias, earlier, tab, part, xs, my):
    _, _, c, y, zt = field.shape
    rows = tab.inner.shape[0]
    args = [recv] + [jnp.asarray(a) for a in (tab.ys, tab.ya, tab.inner, tab.perm, tab.perm_t, tab.rep)] + [point]
    plane = pl.BlockSpec((1, 1, c, y, zt), lambda i: (0, part * xs + i, 0, 0, 0))
    specs = [plane, plane] + [whole(a) for a in args] + [pl.BlockSpec(memory_space=pltpu.SMEM)]
    operands = [field, cot, *args, bias]
    aliases = {}
    if earlier is not None:
        aliases = {len(operands): 0}
        operands.append(earlier)
        specs.append(pl.BlockSpec(memory_space=pl.ANY))
    return pl.pallas_call(
        partial(forward_kernel, earlier is not None),
        grid=(xs,),
        in_specs=specs,
        out_specs=[plane, pl.BlockSpec((1, c, y, zt), lambda i: (i, 0, 0, 0)), whole(recv)],
        out_shape=[jax.ShapeDtypeStruct(field.shape, BF), jax.ShapeDtypeStruct((xs, c, y, zt), BF),
                   jax.ShapeDtypeStruct(recv.shape, BF)],
        scratch_shapes=[pltpu.VMEM((xs * rows, c * my), BF), pltpu.VMEM((xs * rows, c * my), BF),
                        pltpu.VMEM((c * my, 2 * zt), BF), pltpu.VMEM((c * 16, c * 16), BF),
                        pltpu.VMEM((c, y, zt), F32)],
        input_output_aliases=aliases,
        compiler_params=params(),
        name="forward",
    )(*operands)


def final_kernel(aliased, grad, recv, ys, inner, perm_t, rep, point, *refs):
    if aliased:
        refs = refs[1:]
    out, all_in, v_ref, kron, acc = refs
    i = pl.program_id(0)
    c, y, zt = grad.shape[1:]
    my = v_ref.shape[0] // c
    rows = inner.shape[0]

    @pl.when(i == 0)
    def _():
        all_in[...] = dot(perm_t[...], recv[...]).astype(BF)
        expand_point(point, rep, kron, True)

    here = pl.ds(pl.multiple_of(i * rows, rows), rows)
    v_ref[...] = dot(all_in[here, :], inner[...], TN).astype(BF)
    linear_plane(lambda j: grad[0, :, 16 * j:16 * j + 16, :], kron, acc, c, y)
    for g in range(c // 8):
        spectral = synth_group(g, v_ref, ys, my, zt).reshape(8, y, zt)
        out[0, 0, 8 * g:8 * g + 8] = (spectral + acc[8 * g:8 * g + 8]).astype(BF)


def final(grad, recv, point, earlier, shape, tab, part, my):
    xs, c, y, zt = grad.shape
    rows = tab.inner.shape[0]
    args = [recv] + [jnp.asarray(a) for a in (tab.ys, tab.inner, tab.perm_t, tab.rep)] + [point]
    specs = [pl.BlockSpec((1, c, y, zt), lambda i: (i, 0, 0, 0))] + [whole(a) for a in args]
    operands = [grad, *args]
    aliases = {}
    if earlier is not None:
        aliases = {len(operands): 0}
        operands.append(earlier)
        specs.append(pl.BlockSpec(memory_space=pl.ANY))
    return pl.pallas_call(
        partial(final_kernel, earlier is not None),
        grid=(xs,),
        in_specs=specs,
        out_specs=pl.BlockSpec((1, 1, c, y, zt), lambda i: (0, part * xs + i, 0, 0, 0)),
        out_shape=jax.ShapeDtypeStruct(shape, BF),
        scratch_shapes=[pltpu.VMEM((xs * rows, c * my), BF), pltpu.VMEM((c * my, 2 * zt), BF),
                        pltpu.VMEM((c * 16, c * 16), BF), pltpu.VMEM((c, y, zt), F32)],
        input_output_aliases=aliases,
        compiler_params=params(),
        name="final",
    )(*operands)


def exchange(block, n):
    shape = block.shape
    block = block.reshape(n, shape[0] // n, shape[1])
    block = lax.all_to_all(block, "slab", split_axis=0, concat_axis=0, tiled=True)
    return block.reshape(shape)


def samples_of(a, dp):
    return [a] + [
        lax.ppermute(a, "dp", [(j, (j + s) % dp) for j in range(dp)]) for s in range(1, dp)
    ]


def per_device(n, dp, field, cotangent, spectral_weight, point_weight, bias_term):
    _, xl, c, y, zt = field.shape
    ql, mx, my = spectral_weight.shape[:3]
    parts = PARTS if xl % PARTS == 0 else 1
    xs = xl // parts
    tab = Tables(n, xl, c, y, ql, mx, my, parts)
    scale = 1.0 / (n * xl * y * zt)
    recv = [exchange(analyse(field, tab, p, xs, my), n) for p in range(parts)]
    *sent, spec = mix(recv, spectral_weight, tab, my, scale)
    specs = samples_of(spec, dp)
    recv = [exchange(a, n) for a in sent]
    layer, grads, sent = None, [], []
    for p in range(parts):
        layer, grad, out = forward(field, cotangent, recv[p], point_weight, bias_term, layer, tab, p, xs, my)
        grads.append(grad)
        sent.append(exchange(out, n))
    *sent, gspec = back(sent, spectral_weight, tab, my, scale)
    gspecs = samples_of(gspec, dp)
    recv = [exchange(a, n) for a in sent]
    weight_grad = weight_gradient(specs, gspecs, spectral_weight.shape, tab)
    total = None
    for p in range(parts):
        total = final(grads[p], recv[p], point_weight, total, field.shape, tab, p, my)
    return layer, total, weight_grad


def solution(mesh):
    spread = P("dp", "slab", None, None, None)
    modes = P("slab", None, None, None, None)
    return jax.shard_map(
        partial(per_device, mesh.shape["slab"], mesh.shape["dp"]),
        mesh=mesh,
        in_specs=(spread, spread, modes, P(), P()),
        out_specs=(spread, spread, modes),
        check_vma=False,
    )
```

```python
from functools import partial

import jax
import jax.numpy as jnp
import ml_dtypes
import numpy as np
from jax import lax
from jax.experimental import pallas as pl
from jax.experimental.pallas import tpu as pltpu
from jax.sharding import PartitionSpec as P

X = 64
Z = 32
T_SIZE = 16
MZ = 12
MT = 8
PARTS = 1
LIMIT = 52 * 1024 * 1024
BF = jnp.bfloat16
F32 = jnp.float32
NT = (((1,), (1,)), ((), ()))
TN = (((0,), (0,)), ((), ()))


def signed(m):
    i = np.arange(m)
    return np.where(i < m // 2, i, i - m)


def rounded(a):
    return np.asarray(a, np.float32).astype(ml_dtypes.bfloat16)


def waves(modes, length):
    angle = 2.0 * np.pi / length * ((signed(modes)[:, None] * np.arange(length)[None, :]) % length)
    return np.cos(angle), np.sin(angle)


def zt_waves():
    q = np.arange(MZ * MT)
    t = np.arange(Z * T_SIZE)
    total = Z * T_SIZE
    counts = (signed(MZ)[q // MT][:, None] * (t // T_SIZE)[None, :] * T_SIZE
              + (q % MT)[:, None] * (t % T_SIZE)[None, :] * Z) % total
    angle = 2.0 * np.pi / total * counts
    return np.cos(angle), -np.sin(angle)


class Tables:
    def __init__(self, n, xl, c, y, ql, mx, my, parts):
        xs = xl // parts
        i0, i1 = zt_waves()
        rows = np.arange(n * 2 * ql)
        dest, r, j = rows // (2 * ql), rows // ql % 2, rows % ql
        q = dest * ql + j
        first = np.where(r[:, None] == 0, i0[q], i1[q])
        second = np.where(r[:, None] == 0, i1[q], -i0[q])
        self.inner = rounded(np.concatenate([first, second], axis=1))
        cos, sin = waves(my, y)
        g = 4
        eye = np.eye(g)
        self.ya = rounded(np.stack([
            np.einsum("ab,ky->akby", eye, w).reshape(g * my, g * y) for w in (cos, sin)
        ]).reshape(2 * g * my, g * y))
        g = 8
        eye = np.eye(g)
        self.ys = rounded(np.concatenate([
            np.einsum("ab,ky->aybk", eye, w).reshape(g * y, g * my) for w in (cos, sin)
        ], axis=1))
        k = n * xs * 2 * ql
        out = np.arange(k)
        d, rest = out // (xs * 2 * ql), out % (xs * 2 * ql)
        x, w = rest // (2 * ql), rest % (2 * ql)
        src = (x * n + d) * 2 * ql + w
        perm = np.zeros((k, k))
        perm[out, src] = 1
        self.perm = rounded(perm)
        self.perm_t = rounded(perm.T)
        cx, sx = waves(mx, n * xl)
        big = np.zeros((2, 2, mx, n * xl))
        big[0, 0], big[0, 1], big[1, 0], big[1, 1] = cx, sx, -sx, cx
        full = np.einsum("rpkx,qj->qkrxpj", big, np.eye(ql))
        full = full.reshape(ql * mx * 2, n, parts, xs * 2 * ql)
        self.xa = rounded(full.transpose(2, 0, 1, 3).reshape(parts, ql * mx * 2, k))
        self.xs = rounded(full.transpose(2, 1, 3, 0).reshape(parts, k, ql * mx * 2))
        lanes = np.arange(c * my)
        swap = np.zeros((c * my, c * my))
        swap[lanes, lanes % my * c + lanes // my] = 1
        self.swap = rounded(swap)
        self.swap_t = rounded(swap.T)
        tile = np.zeros((c, c * my))
        tile[lanes // my, lanes] = 1
        self.tile = rounded(tile)
        spread = np.zeros((mx * 2 * my, mx * 2))
        spread[np.arange(mx * 2 * my), np.arange(mx * 2 * my) // my] = 1
        self.spread = rounded(spread)
        h = 16
        rep = np.zeros((c * h, c))
        rep[np.arange(c * h), np.arange(c * h) // h] = 1
        self.rep = rounded(rep)


def dot(a, b, dims=None):
    if dims is None:
        return jnp.dot(a, b, preferred_element_type=F32)
    return lax.dot_general(a, b, dims, preferred_element_type=F32)


def whole(a):
    return pl.BlockSpec(a.shape, lambda *_: (0,) * a.ndim)


def analyse_plane(load, ya, inner, v_ref, c, y, my):
    zt = inner.shape[1] // 2
    for g in range(c // 4):
        out = dot(ya[...], load(g).reshape(4 * y, zt)).astype(BF)
        v_ref[4 * my * g:4 * my * (g + 1), :zt] = out[:4 * my]
        v_ref[4 * my * g:4 * my * (g + 1), zt:] = out[4 * my:]
    return dot(inner[...], v_ref[...], NT).astype(BF)


def analyse_kernel(field, ya, inner, perm, out, v_ref, all_ref):
    i, steps = pl.program_id(0), pl.num_programs(0)
    c, y = field.shape[2:4]
    my = v_ref.shape[0] // c
    rows = inner.shape[0]
    spec = analyse_plane(lambda g: field[0, 0, 4 * g:4 * g + 4], ya, inner, v_ref, c, y, my)
    all_ref[pl.ds(pl.multiple_of(i * rows, rows), rows), :] = spec

    @pl.when(i == steps - 1)
    def _():
        out[...] = dot(perm[...], all_ref[...]).astype(BF)


def params():
    return pltpu.CompilerParams(vmem_limit_bytes=LIMIT)


def analyse(field, tab, part, xs, my):
    _, _, c, y, zt = field.shape
    rows = tab.inner.shape[0]
    args = [jnp.asarray(tab.ya), jnp.asarray(tab.inner), jnp.asarray(tab.perm)]
    return pl.pallas_call(
        analyse_kernel,
        grid=(xs,),
        in_specs=[pl.BlockSpec((1, 1, c, y, zt), lambda i: (0, part * xs + i, 0, 0, 0))] + [whole(a) for a in args],
        out_specs=pl.BlockSpec((xs * rows, c * my), lambda i: (0, 0)),
        out_shape=jax.ShapeDtypeStruct((xs * rows, c * my), BF),
        scratch_shapes=[pltpu.VMEM((c * my, 2 * zt), BF), pltpu.VMEM((xs * rows, c * my), BF)],
        compiler_params=params(),
        name="analyse",
    )(field, *args)


def row_mask(rows, lanes, my, by_minor, c):
    row = lax.broadcasted_iota(jnp.int32, (rows, lanes), 0) % my
    lane = lax.broadcasted_iota(jnp.int32, (rows, lanes), 1)
    return row == (lane % my if by_minor else lane // c)


def mix_kernel(parts, my, scale, *refs):
    recv = refs[:parts]
    w, xa, xs, swap, tile, spread = refs[parts:parts + 6]
    outs = refs[parts + 6:2 * parts + 6]
    spec_out, spec, mixed, both = refs[2 * parts + 6:]
    i, steps = pl.program_id(0), pl.num_programs(0)
    c, mx = w.shape[3], w.shape[1]
    lanes = c * my

    @pl.when(i == 0)
    def _():
        total = dot(xa[0], recv[0][...])
        for p in range(1, parts):
            total += dot(xa[p], recv[p][...])
        spec[...] = dot(total.astype(BF), swap[...]).astype(BF)
        spec_out[...] = spec[...]

    here = pl.ds(pl.multiple_of(i * mx * 2, mx * 2), mx * 2)
    rep = dot(spread[...], spec[here, :])
    block = jnp.where(row_mask(mx * 2 * my, lanes, my, False, c), rep, 0.0).astype(BF)
    for k in range(mx):
        both[2 * my * k:2 * my * (k + 1), :] = dot(
            block[2 * my * k:2 * my * (k + 1)], w[0, k].reshape(lanes, 2 * c))
    b = both[...].reshape(mx, 2, my, 2 * c)
    b0, b1 = b[:, 0], b[:, 1]
    real = b0[..., :c] - b1[..., c:]
    imag = b0[..., c:] + b1[..., :c]
    small = jnp.stack([real, imag], axis=1).reshape(mx * 2 * my, c).astype(BF)
    wide = dot(small, tile[...])
    wide = jnp.where(row_mask(mx * 2 * my, lanes, my, True, c), wide, 0.0).astype(BF)
    mixed[here, :] = dot(spread[...], wide, TN).astype(BF)

    @pl.when(i == steps - 1)
    def _():
        for p in range(parts):
            outs[p][...] = (dot(xs[p], mixed[...]) * scale).astype(BF)


def mix(recv, weight, tab, my, scale):
    parts = len(recv)
    ql, mx, _, c, _ = weight.shape
    lanes = c * my
    args = [jnp.asarray(a) for a in (tab.xa, tab.xs, tab.swap, tab.tile, tab.spread)]
    rows = ql * mx * 2
    out_shape = [jax.ShapeDtypeStruct(r.shape, BF) for r in recv] + [jax.ShapeDtypeStruct((rows, lanes), BF)]
    return pl.pallas_call(
        partial(mix_kernel, parts, my, scale),
        grid=(ql,),
        in_specs=[whole(r) for r in recv]
        + [pl.BlockSpec((1, mx, my, c, 2 * c), lambda i: (i, 0, 0, 0, 0))]
        + [whole(a) for a in args],
        out_specs=[whole(a) for a in out_shape],
        out_shape=out_shape,
        scratch_shapes=[pltpu.VMEM((rows, lanes), BF), pltpu.VMEM((rows, lanes), BF),
                        pltpu.VMEM((mx * 2 * my, 2 * c), F32)],
        compiler_params=params(),
        name="mix",
    )(*recv, weight, *args)


def pair_rows(g, tile, spread, mask, mx, my, c):
    rep = jnp.where(mask, dot(spread[...], g), 0.0).astype(BF)
    small = dot(rep, tile[...], NT).reshape(mx, 2, my, c)
    real, imag = small[:, 0], small[:, 1]
    first = jnp.concatenate([real, imag], axis=-1)
    second = jnp.concatenate([imag, -real], axis=-1)
    return jnp.stack([first, second], axis=1).reshape(mx * 2 * my, 2 * c).astype(BF)


def back_kernel(parts, my, scale, *refs):
    recv = refs[:parts]
    w, xa, xs, swap_t, tile, spread = refs[parts:parts + 6]
    outs = refs[parts + 6:2 * parts + 6]
    spec_out, spec, mixed, wide = refs[2 * parts + 6:]
    i, steps = pl.program_id(0), pl.num_programs(0)
    c, mx = w.shape[3], w.shape[1]
    lanes = c * my

    @pl.when(i == 0)
    def _():
        total = dot(xa[0], recv[0][...])
        for p in range(1, parts):
            total += dot(xa[p], recv[p][...])
        spec[...] = (total * scale).astype(BF)
        spec_out[...] = spec[...]

    here = pl.ds(pl.multiple_of(i * mx * 2, mx * 2), mx * 2)
    mask = row_mask(mx * 2 * my, lanes, my, True, c)
    pair = pair_rows(spec[here, :], tile, spread, mask, mx, my, c)
    block = row_mask(2 * my, lanes, my, False, c)
    for k in range(mx):
        out = dot(pair[2 * my * k:2 * my * (k + 1)], w[0, k].reshape(lanes, 2 * c), NT)
        wide[2 * my * k:2 * my * (k + 1), :] = jnp.where(block, out, 0.0).astype(BF)
    mixed[here, :] = dot(spread[...], wide[...], TN).astype(BF)

    @pl.when(i == steps - 1)
    def _():
        turned = dot(mixed[...], swap_t[...]).astype(BF)
        for p in range(parts):
            outs[p][...] = dot(xs[p], turned).astype(BF)


def back(recv, weight, tab, my, scale):
    parts = len(recv)
    ql, mx, _, c, _ = weight.shape
    lanes = c * my
    args = [jnp.asarray(a) for a in (tab.xa, tab.xs, tab.swap_t, tab.tile, tab.spread)]
    rows = ql * mx * 2
    out_shape = [jax.ShapeDtypeStruct(r.shape, BF) for r in recv] + [jax.ShapeDtypeStruct((rows, lanes), BF)]
    return pl.pallas_call(
        partial(back_kernel, parts, my, scale),
        grid=(ql,),
        in_specs=[whole(r) for r in recv]
        + [pl.BlockSpec((1, mx, my, c, 2 * c), lambda i: (i, 0, 0, 0, 0))]
        + [whole(a) for a in args],
        out_specs=[whole(a) for a in out_shape],
        out_shape=out_shape,
        scratch_shapes=[pltpu.VMEM((rows, lanes), BF), pltpu.VMEM((rows, lanes), BF),
                        pltpu.VMEM((mx * 2 * my, lanes), BF)],
        compiler_params=params(),
        name="back",
    )(*recv, weight, *args)


def weight_kernel(samples, my, *refs):
    specs, grads = refs[:samples], refs[samples:2 * samples]
    tile, spread, out = refs[2 * samples:]
    mx, c = out.shape[1], out.shape[3]
    lanes = c * my
    rows = mx * 2 * my
    minor = row_mask(rows, lanes, my, True, c)
    major = row_mask(rows, lanes, my, False, c)
    blocks, pairs = [], []
    for s in range(samples):
        blocks.append(jnp.where(major, dot(spread[...], specs[s][...]), 0.0).astype(BF))
        pairs.append(pair_rows(grads[s][...], tile, spread, minor, mx, my, c))
    for k in range(mx):
        cut = slice(2 * my * k, 2 * my * (k + 1))
        left = jnp.concatenate([b[cut] for b in blocks], axis=0)
        right = jnp.concatenate([b[cut] for b in pairs], axis=0)
        out[0, k] = dot(left, right, TN).reshape(my, c, 2 * c)


def weight_gradient(specs, grads, shape, tab):
    ql, mx, my, c, _ = shape
    lanes = c * my
    args = [jnp.asarray(tab.tile), jnp.asarray(tab.spread)]
    block = pl.BlockSpec((mx * 2, lanes), lambda i: (i, 0))
    return pl.pallas_call(
        partial(weight_kernel, len(specs), my),
        grid=(ql,),
        in_specs=[block] * (2 * len(specs)) + [whole(a) for a in args],
        out_specs=pl.BlockSpec((1, mx, my, c, 2 * c), lambda i: (i, 0, 0, 0, 0)),
        out_shape=jax.ShapeDtypeStruct(shape, F32),
        compiler_params=params(),
        name="weight_gradient",
    )(*specs, *grads, *args)


def expand_point(point, rep, kron, transposed):
    half = dot(rep[...], point[...], (((1,), (0 if not transposed else 1,)), ((), ()))).astype(BF)
    full = dot(half, rep[...], NT)
    n = full.shape[0]
    row = lax.broadcasted_iota(jnp.int32, (n, n), 0) % 16
    lane = lax.broadcasted_iota(jnp.int32, (n, n), 1) % 16
    kron[...] = jnp.where(row == lane, full, 0.0).astype(BF)


def linear_plane(load, kron, acc, c, y):
    for j in range(y // 16):
        block = load(j)
        zt = block.shape[-1]
        acc[:, 16 * j:16 * j + 16, :] = dot(kron[...], block.reshape(c * 16, zt)).reshape(c, 16, zt)


def synth_group(g, v, ys, my, zt):
    rows = 8 * my
    cut = slice(rows * g, rows * (g + 1))
    both = jnp.concatenate([v[cut, :zt], v[cut, zt:]], axis=0)
    return dot(ys[...], both)


def forward_kernel(aliased, field, cot, recv, ys, ya, inner, perm, perm_t, rep, point, bias, *refs):
    if aliased:
        refs = refs[1:]
    layer, grad, out, all_in, all_out, v_ref, kron, acc = refs
    i, steps = pl.program_id(0), pl.num_programs(0)
    c, y, zt = field.shape[2:]
    my = v_ref.shape[0] // c
    rows = inner.shape[0]

    @pl.when(i == 0)
    def _():
        all_in[...] = dot(perm_t[...], recv[...]).astype(BF)
        expand_point(point, rep, kron, False)

    here = pl.ds(pl.multiple_of(i * rows, rows), rows)
    v_ref[...] = dot(all_in[here, :], inner[...], TN).astype(BF)
    linear_plane(lambda j: field[0, 0, :, 16 * j:16 * j + 16, :], kron, acc, c, y)
    k0 = float(np.sqrt(2.0 / np.pi))
    k1 = k0 * 0.044715
    for g in range(c // 8):
        spectral = synth_group(g, v_ref, ys, my, zt)
        for h in range(8):
            ch = 8 * g + h
            pre = spectral[y * h:y * (h + 1)] + (acc[ch] + bias[ch])
            sq = pre * pre
            th = jnp.tanh(pre * (k0 + k1 * sq))
            cdf = 0.5 + 0.5 * th
            layer[0, 0, ch] = (pre * cdf).astype(BF)
            slope = cdf + (0.5 * pre) * ((1.0 - th * th) * (k0 + (3.0 * k1) * sq))
            grad[0, ch] = (cot[0, 0, ch].astype(F32) * slope).astype(BF)
    all_out[here, :] = analyse_plane(lambda g: grad[0, 4 * g:4 * g + 4], ya, inner, v_ref, c, y, my)

    @pl.when(i == steps - 1)
    def _():
        out[...] = dot(perm[...], all_out[...]).astype(BF)


def forward(field, cot, recv, point, bias, earlier, tab, part, xs, my):
    _, _, c, y, zt = field.shape
    rows = tab.inner.shape[0]
    args = [recv] + [jnp.asarray(a) for a in (tab.ys, tab.ya, tab.inner, tab.perm, tab.perm_t, tab.rep)] + [point]
    plane = pl.BlockSpec((1, 1, c, y, zt), lambda i: (0, part * xs + i, 0, 0, 0))
    specs = [plane, plane] + [whole(a) for a in args] + [pl.BlockSpec(memory_space=pltpu.SMEM)]
    operands = [field, cot, *args, bias]
    aliases = {}
    if earlier is not None:
        aliases = {len(operands): 0}
        operands.append(earlier)
        specs.append(pl.BlockSpec(memory_space=pl.ANY))
    return pl.pallas_call(
        partial(forward_kernel, earlier is not None),
        grid=(xs,),
        in_specs=specs,
        out_specs=[plane, pl.BlockSpec((1, c, y, zt), lambda i: (i, 0, 0, 0)), whole(recv)],
        out_shape=[jax.ShapeDtypeStruct(field.shape, BF), jax.ShapeDtypeStruct((xs, c, y, zt), BF),
                   jax.ShapeDtypeStruct(recv.shape, BF)],
        scratch_shapes=[pltpu.VMEM((xs * rows, c * my), BF), pltpu.VMEM((xs * rows, c * my), BF),
                        pltpu.VMEM((c * my, 2 * zt), BF), pltpu.VMEM((c * 16, c * 16), BF),
                        pltpu.VMEM((c, y, zt), F32)],
        input_output_aliases=aliases,
        compiler_params=params(),
        name="forward",
    )(*operands)


def final_kernel(aliased, grad, recv, ys, inner, perm_t, rep, point, *refs):
    if aliased:
        refs = refs[1:]
    out, all_in, v_ref, kron, acc = refs
    i = pl.program_id(0)
    c, y, zt = grad.shape[1:]
    my = v_ref.shape[0] // c
    rows = inner.shape[0]

    @pl.when(i == 0)
    def _():
        all_in[...] = dot(perm_t[...], recv[...]).astype(BF)
        expand_point(point, rep, kron, True)

    here = pl.ds(pl.multiple_of(i * rows, rows), rows)
    v_ref[...] = dot(all_in[here, :], inner[...], TN).astype(BF)
    linear_plane(lambda j: grad[0, :, 16 * j:16 * j + 16, :], kron, acc, c, y)
    for g in range(c // 8):
        spectral = synth_group(g, v_ref, ys, my, zt).reshape(8, y, zt)
        out[0, 0, 8 * g:8 * g + 8] = (spectral + acc[8 * g:8 * g + 8]).astype(BF)


def final(grad, recv, point, earlier, shape, tab, part, my):
    xs, c, y, zt = grad.shape
    rows = tab.inner.shape[0]
    args = [recv] + [jnp.asarray(a) for a in (tab.ys, tab.inner, tab.perm_t, tab.rep)] + [point]
    specs = [pl.BlockSpec((1, c, y, zt), lambda i: (i, 0, 0, 0))] + [whole(a) for a in args]
    operands = [grad, *args]
    aliases = {}
    if earlier is not None:
        aliases = {len(operands): 0}
        operands.append(earlier)
        specs.append(pl.BlockSpec(memory_space=pl.ANY))
    return pl.pallas_call(
        partial(final_kernel, earlier is not None),
        grid=(xs,),
        in_specs=specs,
        out_specs=pl.BlockSpec((1, 1, c, y, zt), lambda i: (0, part * xs + i, 0, 0, 0)),
        out_shape=jax.ShapeDtypeStruct(shape, BF),
        scratch_shapes=[pltpu.VMEM((xs * rows, c * my), BF), pltpu.VMEM((c * my, 2 * zt), BF),
                        pltpu.VMEM((c * 16, c * 16), BF), pltpu.VMEM((c, y, zt), F32)],
        input_output_aliases=aliases,
        compiler_params=params(),
        name="final",
    )(*operands)


def swap_kernel(n, src, dst, send, recv, own):
    me = lax.axis_index("slab")
    barrier = pltpu.get_barrier_semaphore()
    for k in range(1, n):
        pl.semaphore_signal(barrier, inc=1, device_id={"slab": lax.rem(me + k, n)},
                            device_id_type=pl.DeviceIdType.MESH)
    local = pltpu.make_async_copy(src.at[me], dst.at[me], own)
    local.start()
    pl.semaphore_wait(barrier, n - 1)
    copies = []
    for k in range(1, n):
        to = lax.rem(me + k, n)
        copies.append(pltpu.make_async_remote_copy(
            src_ref=src.at[to], dst_ref=dst.at[me], send_sem=send.at[k], recv_sem=recv.at[k],
            device_id={"slab": to}, device_id_type=pl.DeviceIdType.MESH))
        copies[-1].start()
    local.wait()
    for copy in copies:
        copy.wait()


def push(block, n):
    shape = block.shape
    block = block.reshape(n, shape[0] // n, shape[1])
    out = pl.pallas_call(
        partial(swap_kernel, n),
        in_specs=[pl.BlockSpec(memory_space=pltpu.VMEM)],
        out_specs=pl.BlockSpec(memory_space=pltpu.VMEM),
        out_shape=jax.ShapeDtypeStruct(block.shape, BF),
        scratch_shapes=[pltpu.SemaphoreType.DMA((n,)), pltpu.SemaphoreType.DMA((n,)), pltpu.SemaphoreType.DMA],
        compiler_params=pltpu.CompilerParams(collective_id=0, has_side_effects=True, vmem_limit_bytes=16 * 1024 * 1024),
        name="push",
    )(block)
    return out.reshape(shape)


def exchange(block, n):
    shape = block.shape
    block = block.reshape(n, shape[0] // n, shape[1])
    block = lax.all_to_all(block, "slab", split_axis=0, concat_axis=0, tiled=True)
    return block.reshape(shape)


def samples_of(a, dp):
    return [a] + [
        lax.ppermute(a, "dp", [(j, (j + s) % dp) for j in range(dp)]) for s in range(1, dp)
    ]


def per_device(n, dp, field, cotangent, spectral_weight, point_weight, bias_term):
    _, xl, c, y, zt = field.shape
    ql, mx, my = spectral_weight.shape[:3]
    parts = PARTS if xl % PARTS == 0 else 1
    xs = xl // parts
    tab = Tables(n, xl, c, y, ql, mx, my, parts)
    scale = 1.0 / (n * xl * y * zt)
    recv = [push(analyse(field, tab, p, xs, my), n) for p in range(parts)]
    *sent, spec = mix(recv, spectral_weight, tab, my, scale)
    specs = samples_of(spec, dp)
    recv = [push(a, n) for a in sent]
    layer, grads, sent = None, [], []
    for p in range(parts):
        layer, grad, out = forward(field, cotangent, recv[p], point_weight, bias_term, layer, tab, p, xs, my)
        grads.append(grad)
        sent.append(push(out, n))
    *sent, gspec = back(sent, spectral_weight, tab, my, scale)
    gspecs = samples_of(gspec, dp)
    recv = [exchange(a, n) for a in sent]
    weight_grad = weight_gradient(specs, gspecs, spectral_weight.shape, tab)
    total = None
    for p in range(parts):
        total = final(grads[p], recv[p], point_weight, total, field.shape, tab, p, my)
    return layer, total, weight_grad


def solution(mesh):
    spread = P("dp", "slab", None, None, None)
    modes = P("slab", None, None, None, None)
    return jax.shard_map(
        partial(per_device, mesh.shape["slab"], mesh.shape["dp"]),
        mesh=mesh,
        in_specs=(spread, spread, modes, P(), P()),
        out_specs=(spread, spread, modes),
        check_vma=False,
    )
```

```python
from functools import partial

import jax
import jax.numpy as jnp
import ml_dtypes
import numpy as np
from jax import lax
from jax.experimental import pallas as pl
from jax.experimental.pallas import tpu as pltpu
from jax.sharding import PartitionSpec as P

X = 64
Z = 32
T_SIZE = 16
MZ = 12
MT = 8
PARTS = 1
LIMIT = 52 * 1024 * 1024
BF = jnp.bfloat16
F32 = jnp.float32
NT = (((1,), (1,)), ((), ()))
TN = (((0,), (0,)), ((), ()))


def signed(m):
    i = np.arange(m)
    return np.where(i < m // 2, i, i - m)


def rounded(a):
    return np.asarray(a, np.float32).astype(ml_dtypes.bfloat16)


def waves(modes, length):
    angle = 2.0 * np.pi / length * ((signed(modes)[:, None] * np.arange(length)[None, :]) % length)
    return np.cos(angle), np.sin(angle)


def zt_waves():
    q = np.arange(MZ * MT)
    t = np.arange(Z * T_SIZE)
    total = Z * T_SIZE
    counts = (signed(MZ)[q // MT][:, None] * (t // T_SIZE)[None, :] * T_SIZE
              + (q % MT)[:, None] * (t % T_SIZE)[None, :] * Z) % total
    angle = 2.0 * np.pi / total * counts
    return np.cos(angle), -np.sin(angle)


class Tables:
    def __init__(self, n, xl, c, y, ql, mx, my, parts):
        xs = xl // parts
        i0, i1 = zt_waves()
        rows = np.arange(n * 2 * ql)
        dest, r, j = rows // (2 * ql), rows // ql % 2, rows % ql
        q = dest * ql + j
        first = np.where(r[:, None] == 0, i0[q], i1[q])
        second = np.where(r[:, None] == 0, i1[q], -i0[q])
        self.inner = rounded(np.concatenate([first, second], axis=1))
        cos, sin = waves(my, y)
        g = 4
        eye = np.eye(g)
        self.ya = rounded(np.stack([
            np.einsum("ab,ky->akby", eye, w).reshape(g * my, g * y) for w in (cos, sin)
        ]).reshape(2 * g * my, g * y))
        g = 8
        eye = np.eye(g)
        self.ys = rounded(np.concatenate([
            np.einsum("ab,ky->aybk", eye, w).reshape(g * y, g * my) for w in (cos, sin)
        ], axis=1))
        k = n * xs * 2 * ql
        out = np.arange(k)
        d, rest = out // (xs * 2 * ql), out % (xs * 2 * ql)
        x, w = rest // (2 * ql), rest % (2 * ql)
        src = (x * n + d) * 2 * ql + w
        perm = np.zeros((k, k))
        perm[out, src] = 1
        self.perm = rounded(perm)
        self.perm_t = rounded(perm.T)
        cx, sx = waves(mx, n * xl)
        big = np.zeros((2, 2, mx, n * xl))
        big[0, 0], big[0, 1], big[1, 0], big[1, 1] = cx, sx, -sx, cx
        full = np.einsum("rpkx,qj->qkrxpj", big, np.eye(ql))
        full = full.reshape(ql * mx * 2, n, parts, xs * 2 * ql)
        self.xa = rounded(full.transpose(2, 0, 1, 3).reshape(parts, ql * mx * 2, k))
        self.xs = rounded(full.transpose(2, 1, 3, 0).reshape(parts, k, ql * mx * 2))
        lanes = np.arange(c * my)
        swap = np.zeros((c * my, c * my))
        swap[lanes, lanes % my * c + lanes // my] = 1
        self.swap = rounded(swap)
        self.swap_t = rounded(swap.T)
        tile = np.zeros((c, c * my))
        tile[lanes // my, lanes] = 1
        self.tile = rounded(tile)
        spread = np.zeros((mx * 2 * my, mx * 2))
        spread[np.arange(mx * 2 * my), np.arange(mx * 2 * my) // my] = 1
        self.spread = rounded(spread)
        h = 16
        rep = np.zeros((c * h, c))
        rep[np.arange(c * h), np.arange(c * h) // h] = 1
        self.rep = rounded(rep)


def dot(a, b, dims=None):
    if dims is None:
        return jnp.dot(a, b, preferred_element_type=F32)
    return lax.dot_general(a, b, dims, preferred_element_type=F32)


def whole(a):
    return pl.BlockSpec(a.shape, lambda *_: (0,) * a.ndim)


def analyse_plane(load, ya, inner, v_ref, c, y, my):
    zt = inner.shape[1] // 2
    for g in range(c // 4):
        out = dot(ya[...], load(g).reshape(4 * y, zt)).astype(BF)
        v_ref[4 * my * g:4 * my * (g + 1), :zt] = out[:4 * my]
        v_ref[4 * my * g:4 * my * (g + 1), zt:] = out[4 * my:]
    return dot(inner[...], v_ref[...], NT).astype(BF)


def analyse_kernel(field, ya, inner, perm, out, v_ref, all_ref):
    i, steps = pl.program_id(0), pl.num_programs(0)
    c, y = field.shape[2:4]
    my = v_ref.shape[0] // c
    rows = inner.shape[0]
    spec = analyse_plane(lambda g: field[0, 0, 4 * g:4 * g + 4], ya, inner, v_ref, c, y, my)
    all_ref[pl.ds(pl.multiple_of(i * rows, rows), rows), :] = spec

    @pl.when(i == steps - 1)
    def _():
        out[...] = dot(perm[...], all_ref[...]).astype(BF)


def params():
    return pltpu.CompilerParams(vmem_limit_bytes=LIMIT)


def analyse(field, tab, part, xs, my):
    _, _, c, y, zt = field.shape
    rows = tab.inner.shape[0]
    args = [jnp.asarray(tab.ya), jnp.asarray(tab.inner), jnp.asarray(tab.perm)]
    return pl.pallas_call(
        analyse_kernel,
        grid=(xs,),
        in_specs=[pl.BlockSpec((1, 1, c, y, zt), lambda i: (0, part * xs + i, 0, 0, 0))] + [whole(a) for a in args],
        out_specs=pl.BlockSpec((xs * rows, c * my), lambda i: (0, 0)),
        out_shape=jax.ShapeDtypeStruct((xs * rows, c * my), BF),
        scratch_shapes=[pltpu.VMEM((c * my, 2 * zt), BF), pltpu.VMEM((xs * rows, c * my), BF)],
        compiler_params=params(),
        name="analyse",
    )(field, *args)


def row_mask(rows, lanes, my, by_minor, c):
    row = lax.broadcasted_iota(jnp.int32, (rows, lanes), 0) % my
    lane = lax.broadcasted_iota(jnp.int32, (rows, lanes), 1)
    return row == (lane % my if by_minor else lane // c)


def mix_kernel(parts, my, scale, *refs):
    recv = refs[:parts]
    w, xa, xs, swap, tile, spread = refs[parts:parts + 6]
    outs = refs[parts + 6:2 * parts + 6]
    spec_out, spec, mixed, both = refs[2 * parts + 6:]
    i, steps = pl.program_id(0), pl.num_programs(0)
    c, mx = w.shape[3], w.shape[1]
    lanes = c * my

    @pl.when(i == 0)
    def _():
        total = dot(xa[0], recv[0][...])
        for p in range(1, parts):
            total += dot(xa[p], recv[p][...])
        spec[...] = dot(total.astype(BF), swap[...]).astype(BF)
        spec_out[...] = spec[...]

    here = pl.ds(pl.multiple_of(i * mx * 2, mx * 2), mx * 2)
    rep = dot(spread[...], spec[here, :])
    block = jnp.where(row_mask(mx * 2 * my, lanes, my, False, c), rep, 0.0).astype(BF)
    for k in range(mx):
        both[2 * my * k:2 * my * (k + 1), :] = dot(
            block[2 * my * k:2 * my * (k + 1)], w[0, k].reshape(lanes, 2 * c))
    b = both[...].reshape(mx, 2, my, 2 * c)
    b0, b1 = b[:, 0], b[:, 1]
    real = b0[..., :c] - b1[..., c:]
    imag = b0[..., c:] + b1[..., :c]
    small = jnp.stack([real, imag], axis=1).reshape(mx * 2 * my, c).astype(BF)
    wide = dot(small, tile[...])
    wide = jnp.where(row_mask(mx * 2 * my, lanes, my, True, c), wide, 0.0).astype(BF)
    mixed[here, :] = dot(spread[...], wide, TN).astype(BF)

    @pl.when(i == steps - 1)
    def _():
        for p in range(parts):
            outs[p][...] = (dot(xs[p], mixed[...]) * scale).astype(BF)


def mix(recv, weight, tab, my, scale):
    parts = len(recv)
    ql, mx, _, c, _ = weight.shape
    lanes = c * my
    args = [jnp.asarray(a) for a in (tab.xa, tab.xs, tab.swap, tab.tile, tab.spread)]
    rows = ql * mx * 2
    out_shape = [jax.ShapeDtypeStruct(r.shape, BF) for r in recv] + [jax.ShapeDtypeStruct((rows, lanes), BF)]
    return pl.pallas_call(
        partial(mix_kernel, parts, my, scale),
        grid=(ql,),
        in_specs=[whole(r) for r in recv]
        + [pl.BlockSpec((1, mx, my, c, 2 * c), lambda i: (i, 0, 0, 0, 0))]
        + [whole(a) for a in args],
        out_specs=[whole(a) for a in out_shape],
        out_shape=out_shape,
        scratch_shapes=[pltpu.VMEM((rows, lanes), BF), pltpu.VMEM((rows, lanes), BF),
                        pltpu.VMEM((mx * 2 * my, 2 * c), F32)],
        compiler_params=params(),
        name="mix",
    )(*recv, weight, *args)


def pair_rows(g, tile, spread, mask, mx, my, c):
    rep = jnp.where(mask, dot(spread[...], g), 0.0).astype(BF)
    small = dot(rep, tile[...], NT).reshape(mx, 2, my, c)
    real, imag = small[:, 0], small[:, 1]
    first = jnp.concatenate([real, imag], axis=-1)
    second = jnp.concatenate([imag, -real], axis=-1)
    return jnp.stack([first, second], axis=1).reshape(mx * 2 * my, 2 * c).astype(BF)


def back_kernel(parts, my, scale, *refs):
    recv = refs[:parts]
    w, xa, xs, swap_t, tile, spread = refs[parts:parts + 6]
    outs = refs[parts + 6:2 * parts + 6]
    spec_out, spec, mixed, wide = refs[2 * parts + 6:]
    i, steps = pl.program_id(0), pl.num_programs(0)
    c, mx = w.shape[3], w.shape[1]
    lanes = c * my

    @pl.when(i == 0)
    def _():
        total = dot(xa[0], recv[0][...])
        for p in range(1, parts):
            total += dot(xa[p], recv[p][...])
        spec[...] = (total * scale).astype(BF)
        spec_out[...] = spec[...]

    here = pl.ds(pl.multiple_of(i * mx * 2, mx * 2), mx * 2)
    mask = row_mask(mx * 2 * my, lanes, my, True, c)
    pair = pair_rows(spec[here, :], tile, spread, mask, mx, my, c)
    block = row_mask(2 * my, lanes, my, False, c)
    for k in range(mx):
        out = dot(pair[2 * my * k:2 * my * (k + 1)], w[0, k].reshape(lanes, 2 * c), NT)
        wide[2 * my * k:2 * my * (k + 1), :] = jnp.where(block, out, 0.0).astype(BF)
    mixed[here, :] = dot(spread[...], wide[...], TN).astype(BF)

    @pl.when(i == steps - 1)
    def _():
        turned = dot(mixed[...], swap_t[...]).astype(BF)
        for p in range(parts):
            outs[p][...] = dot(xs[p], turned).astype(BF)


def back(recv, weight, tab, my, scale):
    parts = len(recv)
    ql, mx, _, c, _ = weight.shape
    lanes = c * my
    args = [jnp.asarray(a) for a in (tab.xa, tab.xs, tab.swap_t, tab.tile, tab.spread)]
    rows = ql * mx * 2
    out_shape = [jax.ShapeDtypeStruct(r.shape, BF) for r in recv] + [jax.ShapeDtypeStruct((rows, lanes), BF)]
    return pl.pallas_call(
        partial(back_kernel, parts, my, scale),
        grid=(ql,),
        in_specs=[whole(r) for r in recv]
        + [pl.BlockSpec((1, mx, my, c, 2 * c), lambda i: (i, 0, 0, 0, 0))]
        + [whole(a) for a in args],
        out_specs=[whole(a) for a in out_shape],
        out_shape=out_shape,
        scratch_shapes=[pltpu.VMEM((rows, lanes), BF), pltpu.VMEM((rows, lanes), BF),
                        pltpu.VMEM((mx * 2 * my, lanes), BF)],
        compiler_params=params(),
        name="back",
    )(*recv, weight, *args)


def weight_kernel(samples, my, *refs):
    specs, grads = refs[:samples], refs[samples:2 * samples]
    tile, spread, out = refs[2 * samples:]
    mx, c = out.shape[1], out.shape[3]
    lanes = c * my
    rows = mx * 2 * my
    minor = row_mask(rows, lanes, my, True, c)
    major = row_mask(rows, lanes, my, False, c)
    blocks, pairs = [], []
    for s in range(samples):
        blocks.append(jnp.where(major, dot(spread[...], specs[s][...]), 0.0).astype(BF))
        pairs.append(pair_rows(grads[s][...], tile, spread, minor, mx, my, c))
    for k in range(mx):
        cut = slice(2 * my * k, 2 * my * (k + 1))
        left = jnp.concatenate([b[cut] for b in blocks], axis=0)
        right = jnp.concatenate([b[cut] for b in pairs], axis=0)
        out[0, k] = dot(left, right, TN).reshape(my, c, 2 * c)


def weight_gradient(specs, grads, shape, tab):
    ql, mx, my, c, _ = shape
    lanes = c * my
    args = [jnp.asarray(tab.tile), jnp.asarray(tab.spread)]
    block = pl.BlockSpec((mx * 2, lanes), lambda i: (i, 0))
    return pl.pallas_call(
        partial(weight_kernel, len(specs), my),
        grid=(ql,),
        in_specs=[block] * (2 * len(specs)) + [whole(a) for a in args],
        out_specs=pl.BlockSpec((1, mx, my, c, 2 * c), lambda i: (i, 0, 0, 0, 0)),
        out_shape=jax.ShapeDtypeStruct(shape, F32),
        compiler_params=params(),
        name="weight_gradient",
    )(*specs, *grads, *args)


def expand_point(point, rep, kron, transposed):
    half = dot(rep[...], point[...], (((1,), (0 if not transposed else 1,)), ((), ()))).astype(BF)
    full = dot(half, rep[...], NT)
    n = full.shape[0]
    row = lax.broadcasted_iota(jnp.int32, (n, n), 0) % 16
    lane = lax.broadcasted_iota(jnp.int32, (n, n), 1) % 16
    kron[...] = jnp.where(row == lane, full, 0.0).astype(BF)


def linear_plane(load, kron, acc, c, y):
    for j in range(y // 16):
        block = load(j)
        zt = block.shape[-1]
        acc[:, 16 * j:16 * j + 16, :] = dot(kron[...], block.reshape(c * 16, zt)).reshape(c, 16, zt)


def synth_group(g, v, ys, my, zt):
    rows = 8 * my
    cut = slice(rows * g, rows * (g + 1))
    both = jnp.concatenate([v[cut, :zt], v[cut, zt:]], axis=0)
    return dot(ys[...], both)


def forward_kernel(aliased, field, cot, recv, ys, ya, inner, perm, perm_t, rep, point, bias, *refs):
    if aliased:
        refs = refs[1:]
    layer, grad, out, all_in, all_out, v_ref, kron, acc = refs
    i, steps = pl.program_id(0), pl.num_programs(0)
    c, y, zt = field.shape[2:]
    my = v_ref.shape[0] // c
    rows = inner.shape[0]

    @pl.when(i == 0)
    def _():
        all_in[...] = dot(perm_t[...], recv[...]).astype(BF)
        expand_point(point, rep, kron, False)

    here = pl.ds(pl.multiple_of(i * rows, rows), rows)
    v_ref[...] = dot(all_in[here, :], inner[...], TN).astype(BF)
    linear_plane(lambda j: field[0, 0, :, 16 * j:16 * j + 16, :], kron, acc, c, y)
    k0 = float(np.sqrt(2.0 / np.pi))
    k1 = k0 * 0.044715
    for g in range(c // 8):
        spectral = synth_group(g, v_ref, ys, my, zt)
        for h in range(8):
            ch = 8 * g + h
            pre = spectral[y * h:y * (h + 1)] + (acc[ch] + bias[ch])
            sq = pre * pre
            th = jnp.tanh(pre * (k0 + k1 * sq))
            cdf = 0.5 + 0.5 * th
            layer[0, 0, ch] = (pre * cdf).astype(BF)
            slope = cdf + (0.5 * pre) * ((1.0 - th * th) * (k0 + (3.0 * k1) * sq))
            grad[0, ch] = (cot[0, 0, ch].astype(F32) * slope).astype(BF)
    all_out[here, :] = analyse_plane(lambda g: grad[0, 4 * g:4 * g + 4], ya, inner, v_ref, c, y, my)

    @pl.when(i == steps - 1)
    def _():
        out[...] = dot(perm[...], all_out[...]).astype(BF)


def forward(field, cot, recv, point, bias, earlier, tab, part, xs, my):
    _, _, c, y, zt = field.shape
    rows = tab.inner.shape[0]
    args = [recv] + [jnp.asarray(a) for a in (tab.ys, tab.ya, tab.inner, tab.perm, tab.perm_t, tab.rep)] + [point]
    plane = pl.BlockSpec((1, 1, c, y, zt), lambda i: (0, part * xs + i, 0, 0, 0))
    specs = [plane, plane] + [whole(a) for a in args] + [pl.BlockSpec(memory_space=pltpu.SMEM)]
    operands = [field, cot, *args, bias]
    aliases = {}
    if earlier is not None:
        aliases = {len(operands): 0}
        operands.append(earlier)
        specs.append(pl.BlockSpec(memory_space=pl.ANY))
    return pl.pallas_call(
        partial(forward_kernel, earlier is not None),
        grid=(xs,),
        in_specs=specs,
        out_specs=[plane, pl.BlockSpec((1, c, y, zt), lambda i: (i, 0, 0, 0)), whole(recv)],
        out_shape=[jax.ShapeDtypeStruct(field.shape, BF), jax.ShapeDtypeStruct((xs, c, y, zt), BF),
                   jax.ShapeDtypeStruct(recv.shape, BF)],
        scratch_shapes=[pltpu.VMEM((xs * rows, c * my), BF), pltpu.VMEM((xs * rows, c * my), BF),
                        pltpu.VMEM((c * my, 2 * zt), BF), pltpu.VMEM((c * 16, c * 16), BF),
                        pltpu.VMEM((c, y, zt), F32)],
        input_output_aliases=aliases,
        compiler_params=params(),
        name="forward",
    )(*operands)


def final_kernel(aliased, grad, recv, ys, inner, perm_t, rep, point, *refs):
    if aliased:
        refs = refs[1:]
    out, all_in, v_ref, kron, acc = refs
    i = pl.program_id(0)
    c, y, zt = grad.shape[1:]
    my = v_ref.shape[0] // c
    rows = inner.shape[0]

    @pl.when(i == 0)
    def _():
        all_in[...] = dot(perm_t[...], recv[...]).astype(BF)
        expand_point(point, rep, kron, True)

    here = pl.ds(pl.multiple_of(i * rows, rows), rows)
    v_ref[...] = dot(all_in[here, :], inner[...], TN).astype(BF)
    linear_plane(lambda j: grad[0, :, 16 * j:16 * j + 16, :], kron, acc, c, y)
    for g in range(c // 8):
        spectral = synth_group(g, v_ref, ys, my, zt).reshape(8, y, zt)
        out[0, 0, 8 * g:8 * g + 8] = (spectral + acc[8 * g:8 * g + 8]).astype(BF)


def final(grad, recv, point, earlier, shape, tab, part, my):
    xs, c, y, zt = grad.shape
    rows = tab.inner.shape[0]
    args = [recv] + [jnp.asarray(a) for a in (tab.ys, tab.inner, tab.perm_t, tab.rep)] + [point]
    specs = [pl.BlockSpec((1, c, y, zt), lambda i: (i, 0, 0, 0))] + [whole(a) for a in args]
    operands = [grad, *args]
    aliases = {}
    if earlier is not None:
        aliases = {len(operands): 0}
        operands.append(earlier)
        specs.append(pl.BlockSpec(memory_space=pl.ANY))
    return pl.pallas_call(
        partial(final_kernel, earlier is not None),
        grid=(xs,),
        in_specs=specs,
        out_specs=pl.BlockSpec((1, 1, c, y, zt), lambda i: (0, part * xs + i, 0, 0, 0)),
        out_shape=jax.ShapeDtypeStruct(shape, BF),
        scratch_shapes=[pltpu.VMEM((xs * rows, c * my), BF), pltpu.VMEM((c * my, 2 * zt), BF),
                        pltpu.VMEM((c * 16, c * 16), BF), pltpu.VMEM((c, y, zt), F32)],
        input_output_aliases=aliases,
        compiler_params=params(),
        name="final",
    )(*operands)


def swap_kernel(n, src, dst, send, recv, own):
    me = lax.axis_index("slab")
    barrier = pltpu.get_barrier_semaphore()
    for k in range(1, n):
        pl.semaphore_signal(barrier, inc=1, device_id={"slab": lax.rem(me + k, n)},
                            device_id_type=pl.DeviceIdType.MESH)
    local = pltpu.make_async_copy(src.at[me], dst.at[me], own)
    local.start()
    pl.semaphore_wait(barrier, n - 1)
    copies = []
    for k in sorted(range(1, n), key=lambda k: abs(2 * k - n)):
        to = lax.rem(me + k, n)
        copies.append(pltpu.make_async_remote_copy(
            src_ref=src.at[to], dst_ref=dst.at[me], send_sem=send.at[k], recv_sem=recv.at[k],
            device_id={"slab": to}, device_id_type=pl.DeviceIdType.MESH))
        copies[-1].start()
    local.wait()
    for copy in copies:
        copy.wait()


def push(block, n):
    shape = block.shape
    block = block.reshape(n, shape[0] // n, shape[1])
    out = pl.pallas_call(
        partial(swap_kernel, n),
        in_specs=[pl.BlockSpec(memory_space=pltpu.VMEM)],
        out_specs=pl.BlockSpec(memory_space=pltpu.VMEM),
        out_shape=jax.ShapeDtypeStruct(block.shape, BF),
        scratch_shapes=[pltpu.SemaphoreType.DMA((n,)), pltpu.SemaphoreType.DMA((n,)), pltpu.SemaphoreType.DMA],
        compiler_params=pltpu.CompilerParams(collective_id=0, has_side_effects=True, vmem_limit_bytes=16 * 1024 * 1024),
        name="push",
    )(block)
    return out.reshape(shape)


def exchange(block, n):
    shape = block.shape
    block = block.reshape(n, shape[0] // n, shape[1])
    block = lax.all_to_all(block, "slab", split_axis=0, concat_axis=0, tiled=True)
    return block.reshape(shape)


def samples_of(a, dp):
    return [a] + [
        lax.ppermute(a, "dp", [(j, (j + s) % dp) for j in range(dp)]) for s in range(1, dp)
    ]


def per_device(n, dp, field, cotangent, spectral_weight, point_weight, bias_term):
    _, xl, c, y, zt = field.shape
    ql, mx, my = spectral_weight.shape[:3]
    parts = PARTS if xl % PARTS == 0 else 1
    xs = xl // parts
    tab = Tables(n, xl, c, y, ql, mx, my, parts)
    scale = 1.0 / (n * xl * y * zt)
    recv = [push(analyse(field, tab, p, xs, my), n) for p in range(parts)]
    *sent, spec = mix(recv, spectral_weight, tab, my, scale)
    specs = samples_of(spec, dp)
    recv = [push(a, n) for a in sent]
    layer, grads, sent = None, [], []
    for p in range(parts):
        layer, grad, out = forward(field, cotangent, recv[p], point_weight, bias_term, layer, tab, p, xs, my)
        grads.append(grad)
        sent.append(push(out, n))
    *sent, gspec = back(sent, spectral_weight, tab, my, scale)
    gspecs = samples_of(gspec, dp)
    recv = [exchange(a, n) for a in sent]
    weight_grad = weight_gradient(specs, gspecs, spectral_weight.shape, tab)
    total = None
    for p in range(parts):
        total = final(grads[p], recv[p], point_weight, total, field.shape, tab, p, my)
    return layer, total, weight_grad


def solution(mesh):
    spread = P("dp", "slab", None, None, None)
    modes = P("slab", None, None, None, None)
    return jax.shard_map(
        partial(per_device, mesh.shape["slab"], mesh.shape["dp"]),
        mesh=mesh,
        in_specs=(spread, spread, modes, P(), P()),
        out_specs=(spread, spread, modes),
        check_vma=False,
    )
```
